32 devices in a mesh: groups: 2 (over y), dp: 16 (over z, x, core).
Axes of the slice: x: 2, y: 2, z: 4, core: 2. Of those that a mesh axis runs over, the one named last changes fastest.
Arguments:
- queries: bfloat16 [96, 128, 2560], P(('groups', 'dp')), parts along dimension 0, may hold values from -50 to 50
- keys: bfloat16 [96, 128, 2560], P(('groups', 'dp')), parts along dimension 0, may hold values from -4 to 4
- values: bfloat16 [96, 128, 2560], P(('groups', 'dp')), parts along dimension 0, may hold values from -6 to 6
- counts: int32 [32], P(('groups', 'dp')), parts along dimension 0, may hold values from 1 to 3, as said below
- neighbours: int32 [96, 3], P(('groups', 'dp')), parts along dimension 0, may hold values from 0 to 5, as said below
- gate_table: float32 [50, 2560], replicated, may hold values from 1 to 8
- step: int32 [1], replicated, may hold values from 0 to 49
- out_weight: bfloat16 [2560, 5120], P(None, 'dp'), may hold values from -0.125 to 0.125
Outputs:
- mixed: bfloat16 [96, 128, 5120], P(('groups', 'dp')), parts along dimension 0
The draws below stay inside these ranges and needn't reach their ends.
There are 2 independent parts, one for each index of `groups`. The reference program is written for one: setup_inputs(seed, part) draws one part's arguments, and reference() takes and returns one part's arrays. A program takes and returns all parts, laid end to end along the dimension named above; an argument that names none is the same for every part. Nothing has to cross between parts.
Inputs may be any that keep to these rules, and one draw needn't show every extreme that they name: `counts`: the live slots of a device come first. Member m holds the devices (m*4 + 4//2 + r) modulo the number of devices, r = 0 to 3, its tile list running through them in that order. Some device holds 3 live tiles. `neighbours`: row t (a tile of device d) names 3 places of device d's extended list: places 0 to 0 are tiles s to s+1 - 1 of device d-1 (around the axis) with s = max(counts[d-1]-1, 0), place 1+j is the device's slot j, places 1 + 3 onward are the first tiles of device d+1 (around the axis), and 5 names no tile. In a live tile's row the first entry is the tile itself and the others name distinct live tiles of the same member or no tile; rows of slots past the device's count name no tile at all.
All inputs are finite; a program needn't handle non-finite values.
Results may differ from the reference program's by a relative error of at most 0.0052.
Values may be sent and summed in bfloat16 or wider, within the bound.
No kernel may reach another device: no remote copies, remote signals or barrier semaphores. Data moves between devices by JAX's collectives and lax.ppermute only.
A program may use at most 192 MiB of HBM per device.

```python
import math
import jax
import jax.numpy as jnp
from jax import lax

D = 5120
HEADS = 20
HEAD_DIM = 128
TILE = 128
HALO = 1
MEMBER_DEVS = 4
STEPS = 50
SLOTS = 3
NB = 3
TILES = 48


def member_layout():
    device_total = TILES // SLOTS
    member_total = device_total // MEMBER_DEVS
    device_ids = jnp.arange(device_total)
    relative = (device_ids - MEMBER_DEVS // 2) % device_total
    member_of = relative // MEMBER_DEVS
    rank_in = relative % MEMBER_DEVS
    member_devices = (jnp.arange(member_total)[:, None] * MEMBER_DEVS + MEMBER_DEVS // 2 + jnp.arange(MEMBER_DEVS)[None, :]) % device_total
    return (member_of, rank_in, member_devices)


def layout_counts(key):
    device_total = TILES // SLOTS
    member_total = device_total // MEMBER_DEVS
    member_of, rank_in, member_devices = member_layout()
    key_level, key_top, key_jitter, key_mask = jax.random.split(jax.random.fold_in(key, 101), 4)
    levels = jax.random.randint(key_level, (member_total,), 1, SLOTS + 1)
    busiest = jax.random.randint(key_top, (), 0, member_total)
    levels = jnp.where(jnp.arange(member_total) == busiest, SLOTS, levels)
    jitter = jax.random.randint(key_jitter, (device_total,), -1, 2)
    counts = jnp.clip(levels[member_of] + jitter, 1, SLOTS)
    busiest_device = (busiest * MEMBER_DEVS + MEMBER_DEVS // 2) % device_total
    counts = jnp.where(jnp.arange(device_total) == busiest_device, SLOTS, counts)
    return (counts.astype(jnp.int32), key_mask)


def draw_counts(key, part):
    return layout_counts(key)[0]


def draw_neighbours(key, part):
    counts, key_mask = layout_counts(key)
    device_total = TILES // SLOTS
    member_of, rank_in, member_devices = member_layout()
    member_counts = counts[member_devices]
    prefix = jnp.cumsum(member_counts, axis=1) - member_counts
    totals = jnp.sum(member_counts, axis=1)
    slot_ids = jnp.arange(SLOTS)
    member_prefix = prefix[member_of]
    own_prefix = jnp.take_along_axis(member_prefix, rank_in[:, None], axis=1)
    position = own_prefix + slot_ids[None, :]
    live = slot_ids[None, :] < counts[:, None]
    sentinel = SLOTS + 2 * HALO
    member_totals = totals[member_of][:, None]
    counts_before = jnp.roll(counts, 1)
    start_before = jnp.maximum(counts_before - HALO, 0)[:, None]
    columns = [jnp.where(live, HALO + slot_ids[None, :], sentinel)]
    for offset in range(-HALO, HALO + 1):
        if offset == 0:
            continue
        target = position + offset
        inside = (target >= 0) & (target < member_totals)
        target_rank = jnp.sum(member_prefix[:, None, :] <= target[:, :, None], axis=2) - 1
        target_rank = jnp.clip(target_rank, 0, MEMBER_DEVS - 1)
        target_slot = target - jnp.take_along_axis(member_prefix, target_rank, axis=1)
        delta = target_rank - rank_in[:, None]
        place = jnp.where(delta == 0, HALO + target_slot, jnp.where(delta == -1, target_slot - start_before, HALO + SLOTS + target_slot))
        present = jax.random.randint(jax.random.fold_in(key_mask, offset + 10), (device_total, SLOTS), 0, 4) != 0
        if offset < 0:
            forced = slot_ids[None, :] == 0
        else:
            forced = slot_ids[None, :] == counts[:, None] - 1
        keep = live & inside & (jnp.abs(delta) <= 1) & (present | forced)
        columns.append(jnp.where(keep, place, sentinel))
    table = jnp.stack(columns, axis=2)
    return table.reshape(TILES, -1).astype(jnp.int32)


def queries_and_keys(key):
    key_query, key_key = jax.random.split(jax.random.fold_in(key, 202))
    channels = HEADS * HEAD_DIM
    full_shape = (TILES, TILE, channels)
    keys_raw = jnp.clip(jax.random.normal(key_key, full_shape, jnp.float32), -4.0, 4.0)
    queries_raw = 2.5 * jnp.clip(jax.random.normal(key_query, full_shape, jnp.float32), -4.0, 4.0)
    queries_raw = jnp.clip(queries_raw, -50.0, 50.0)
    return (queries_raw, keys_raw)


def draw_queries(key, part):
    return queries_and_keys(key)[0].astype(jnp.bfloat16)


def draw_keys(key, part):
    return queries_and_keys(key)[1].astype(jnp.bfloat16)


def level_of(stream_key, shape, cuts, smallest, high):
    def one(axis_at, shards_of):
        draws = jax.random.uniform(jax.random.fold_in(jax.random.fold_in(stream_key, 6), axis_at), (shards_of,), jnp.float32, smallest / len(cuts), high / len(cuts))
        return jnp.repeat(jnp.exp(draws), shape[axis_at] // shards_of).reshape((-1,) + (1,) * (len(shape) - axis_at - 1))

    gain = one(*cuts[0])
    for cut in cuts[1:]:
        gain = gain * one(*cut)
    return gain


def gaussian(key, shape, deviation, bound, cuts=(), kind=jnp.bfloat16):
    values = jax.random.normal(key, shape, jnp.float32) * deviation
    if len(cuts) > 0:
        values = level_of(key, shape, cuts, -0.22, 0.18) * values
    return jnp.clip(values, min=-bound, max=bound).astype(kind)


def setup_inputs(seed: int = 0, part: int = 0) -> dict:
    arg_keys = jax.random.split(jax.random.key(seed), 9)
    own_keys = jax.random.split(jax.random.fold_in(arg_keys[8], part), 9)
    queries = draw_queries(jax.random.fold_in(jax.random.fold_in(arg_keys[8], part), 71), part)
    keys = draw_keys(jax.random.fold_in(jax.random.fold_in(arg_keys[8], part), 71), part)
    values = gaussian(own_keys[2], (TILES, TILE, HEADS * HEAD_DIM), 1.0, 6.0, ((0, 16),))
    counts = draw_counts(jax.random.fold_in(jax.random.fold_in(arg_keys[8], part), 71), part)
    neighbours = draw_neighbours(jax.random.fold_in(jax.random.fold_in(arg_keys[8], part), 71), part)
    gate_table = jnp.clip(jnp.exp(jax.random.uniform(arg_keys[5], (STEPS, HEADS * HEAD_DIM), jnp.float32, math.log(1.0), math.log(8.0))), 1.0, 8.0)
    step = jax.random.randint(arg_keys[6], (1,), 0, STEPS).astype(jnp.int32)
    out_weight = gaussian(arg_keys[7], (HEADS * HEAD_DIM, D), (HEADS * HEAD_DIM) ** -0.5, 0.125, ((1, 16),))
    return dict(queries=queries, keys=keys, values=values, counts=counts, neighbours=neighbours, gate_table=gate_table, step=step, out_weight=out_weight)


masked_score = -1e+30

def attend_tile(query_tile, key_rows, value_rows, key_valid, gate_row):
    query_rows = query_tile.shape[0]
    queries_h = query_tile.astype(jnp.float32).reshape(query_rows, HEADS, HEAD_DIM)
    keys_h = key_rows.astype(jnp.float32).reshape(-1, HEADS, HEAD_DIM)
    values_h = value_rows.astype(jnp.float32).reshape(-1, HEADS, HEAD_DIM)
    scores = jnp.einsum('qhd,khd->hqk', queries_h, keys_h) * (1.0 / math.sqrt(HEAD_DIM))
    scores = jnp.where(key_valid[None, None, :], scores, masked_score)
    row_max = lax.optimization_barrier(jnp.max(scores, axis=-1, keepdims=True))
    raw_weights = jnp.exp(scores - row_max)
    denominator = lax.optimization_barrier(jnp.sum(raw_weights, axis=-1))
    weights = lax.optimization_barrier(raw_weights.astype(jnp.bfloat16)).astype(jnp.float32)
    summed = jnp.einsum('hqk,khd->qhd', weights, values_h)
    summed = summed / jnp.transpose(denominator)[:, :, None]
    return (summed.reshape(query_rows, HEADS * HEAD_DIM) * gate_row[None, :]).astype(jnp.bfloat16)

def reference(queries, keys, values, counts, neighbours, gate_table, step, out_weight):
    channels = HEADS * HEAD_DIM
    device_total = TILES // SLOTS
    block_shape = (device_total, SLOTS, TILE, channels)
    key_blocks = keys.reshape(block_shape)
    value_blocks = values.reshape(block_shape)
    padded_keys = jnp.concatenate([key_blocks[-1:], key_blocks, key_blocks[:1]], axis=0)
    padded_values = jnp.concatenate([value_blocks[-1:], value_blocks, value_blocks[:1]], axis=0)
    counts_int = counts.astype(jnp.int32)
    padded_counts = jnp.concatenate([counts_int[-1:], counts_int, counts_int[:1]])
    query_blocks = queries.reshape(block_shape)
    index_blocks = neighbours.astype(jnp.int32).reshape(device_total, SLOTS, NB)
    gate_row = lax.dynamic_index_in_dim(gate_table, step[0].astype(jnp.int32), 0, keepdims=False)
    zero_tile = jnp.zeros((1, TILE, channels), keys.dtype)
    sentinel = SLOTS + 2 * HALO

    def extend(padded, device, start):
        before = lax.dynamic_slice_in_dim(lax.dynamic_index_in_dim(padded, device, 0, keepdims=False), start, HALO, 0)
        own_tiles = lax.dynamic_index_in_dim(padded, device + 1, 0, keepdims=False)
        after = lax.dynamic_index_in_dim(padded, device + 2, 0, keepdims=False)[:HALO]
        return jnp.concatenate([before, own_tiles, after, zero_tile], axis=0)

    def per_device(device):
        start = jnp.maximum(padded_counts[device] - HALO, 0).astype(jnp.int32)
        ext_keys = extend(padded_keys, device, start)
        ext_values = extend(padded_values, device, start)
        device_queries = lax.dynamic_index_in_dim(query_blocks, device, 0, keepdims=False)
        device_index = lax.dynamic_index_in_dim(index_blocks, device, 0, keepdims=False)
        live_count = padded_counts[device + 1]

        def per_slot(slot_id):
            tile_index = lax.dynamic_index_in_dim(device_index, slot_id, 0, keepdims=False)
            picked_keys = jnp.take(ext_keys, tile_index, axis=0).reshape(-1, channels)
            picked_values = jnp.take(ext_values, tile_index, axis=0).reshape(-1, channels)
            key_valid = jnp.repeat(tile_index != sentinel, TILE)
            query_tile = lax.dynamic_index_in_dim(device_queries, slot_id, 0, keepdims=False)
            computed = attend_tile(query_tile, picked_keys, picked_values, key_valid, gate_row)
            return jnp.where(slot_id < live_count, computed, jnp.zeros_like(computed))
        attended = lax.map(per_slot, jnp.arange(SLOTS, dtype=jnp.int32))
        projected = jnp.dot(attended.reshape(SLOTS * TILE, channels), out_weight, preferred_element_type=jnp.float32)
        return projected.astype(jnp.bfloat16).reshape(SLOTS, TILE, D)
    result = lax.map(per_device, jnp.arange(device_total, dtype=jnp.int32))
    return result.reshape(TILES, TILE, D)
```

```python
import functools
import math

import jax
import jax.numpy as jnp
from jax import lax
from jax.experimental import pallas as pl
from jax.experimental.pallas import tpu as pltpu
from jax.sharding import PartitionSpec as P

HEADS = 20
HALO = 1
MEMBER_DEVS = 4
CORES = 2
COLUMNS = 2

masked_score = -1e30
VMEM_LIMIT = 48 * 1024 * 1024


def attention_kernel(heads, index_ref, count_ref, q_ref, k_ref, v_ref, before_ref, after_ref, gate_ref, o_ref, ext_k, ext_v):
    slots, rows, width = q_ref.shape
    head_dim = width // heads
    places = slots + 2 * HALO
    picks = index_ref.shape[0] // slots
    ext_k[0:HALO] = before_ref[0]
    ext_v[0:HALO] = before_ref[1]
    ext_k[HALO : HALO + slots] = k_ref[...]
    ext_v[HALO : HALO + slots] = v_ref[...]
    ext_k[HALO + slots : places] = after_ref[0]
    ext_v[HALO + slots : places] = after_ref[1]
    for slot in range(slots):

        @pl.when(slot < count_ref[0])
        def _():
            place = [index_ref[slot * picks + j] for j in range(picks)]
            held = [jnp.minimum(p, places - 1) for p in place]
            for h in range(heads):
                at = pl.ds(h * head_dim, head_dim)
                query = q_ref[slot, :, at]
                scores = []
                for j in range(picks):
                    s = lax.dot_general(
                        query,
                        ext_k[held[j], :, at],
                        (((1,), (1,)), ((), ())),
                        preferred_element_type=jnp.float32,
                    ) * (1.0 / math.sqrt(head_dim))
                    scores.append(jnp.where(place[j] < places, s, masked_score))
                scores = jnp.concatenate(scores, axis=1)
                raw = jnp.exp(scores - jnp.max(scores, axis=1, keepdims=True))
                denominator = jnp.sum(raw, axis=1, keepdims=True)
                vals = jnp.concatenate([ext_v[held[j], :, at] for j in range(picks)], axis=0)
                summed = jnp.dot(raw.astype(jnp.bfloat16), vals, preferred_element_type=jnp.float32)
                o_ref[slot, :, at] = (summed / denominator * gate_ref[:, at]).astype(o_ref.dtype)

        @pl.when(slot >= count_ref[0])
        def _():
            o_ref[slot] = jnp.zeros((rows, width), o_ref.dtype)


def attend(queries, keys, values, before, after, neighbours, counts, gate_row):
    slots, rows, channels = queries.shape
    head_dim = channels // HEADS
    heads = 4 if HEADS % 4 == 0 else 1
    width = heads * head_dim
    places = slots + 2 * HALO
    whole = lambda lead: pl.BlockSpec((lead, rows, width), lambda g, *_: (0, 0, g))
    edge = pl.BlockSpec((2, HALO, rows, width), lambda g, *_: (0, 0, 0, g))
    pairs = slots * HEADS * rows * neighbours.shape[1] * rows
    return pl.pallas_call(
        functools.partial(attention_kernel, heads),
        out_shape=jax.ShapeDtypeStruct((slots, rows, channels), jnp.bfloat16),
        grid_spec=pltpu.PrefetchScalarGridSpec(
            num_scalar_prefetch=2,
            grid=(HEADS // heads,),
            in_specs=[whole(slots), whole(slots), whole(slots), edge, edge, pl.BlockSpec((1, width), lambda g, *_: (0, g))],
            out_specs=whole(slots),
            scratch_shapes=[pltpu.VMEM((places, rows, width), jnp.bfloat16)] * 2,
        ),
        compiler_params=pltpu.CompilerParams(vmem_limit_bytes=VMEM_LIMIT),
        cost_estimate=pl.CostEstimate(
            flops=4 * pairs * head_dim, bytes_accessed=2 * 6 * slots * rows * channels, transcendentals=pairs
        ),
        name="attention",
    )(neighbours.reshape(-1), counts, queries, keys, values, before, after, gate_row)


def project_kernel(pieces_of, has_old, scalars, *refs):
    blocks = len(pieces_of)
    n = sum(pieces_of)
    att_ref, pieces, out_ref = refs[0], refs[1 : 1 + n], refs[1 + n + has_old]
    wbuf, obuf, in_sem, out_sem = refs[2 + n + has_old :]
    shard_rows = wbuf.shape[1] // CORES
    core, group = scalars[0], scalars[1]
    copies = []
    at = 0
    for b in range(blocks):
        mine = []
        for i in range(pieces_of[b]):
            rows = pieces[at].shape[0]
            halves = pieces_of[b] // CORES
            owner = core if i < halves else 1 - core
            start = owner * shard_rows
            if halves == 2:
                half = group if i % 2 == 0 else 1 - group
                start = start + half * rows
            start = pl.multiple_of(start, rows)
            mine.append(pltpu.make_async_copy(pieces[at], wbuf.at[b, pl.ds(start, rows)], in_sem.at[b, i]))
            at += 1
        for c in mine:
            c.start()
        copies.append(mine)
    stores = []
    width = wbuf.shape[1]
    for b in range(blocks):
        for c in copies[b]:
            c.wait()
        if b >= 2:
            stores[b - 2].wait()
        done = 0
        while done < width:
            step = min(256, width - done)
            obuf[b % 2, :, done : done + step] = lax.dot_general(
                att_ref[...],
                wbuf[b, done : done + step],
                (((1,), (1,)), ((), ())),
                preferred_element_type=jnp.float32,
            ).astype(obuf.dtype)
            done += step
        where = pl.ds(pl.multiple_of(scalars[2 + b] * width, width), width)
        store = pltpu.make_async_copy(obuf.at[b % 2], out_ref.at[:, where], out_sem.at[b])
        store.start()
        stores.append(store)
    for store in stores[-2:]:
        store.wait()


def project(att, blocks, chips, core, group, columns, old=None):
    rows, channels = att.shape
    pieces = [p for b in blocks for p in b]
    width = sum(p.shape[0] for p in blocks[0])
    has_old = int(old is not None)
    scalars = jnp.stack([core, group] + list(chips)).astype(jnp.int32)
    anywhere = pl.BlockSpec(memory_space=pl.ANY)
    return pl.pallas_call(
        functools.partial(project_kernel, tuple(len(b) for b in blocks), has_old),
        out_shape=jax.ShapeDtypeStruct((rows, columns), jnp.bfloat16),
        grid_spec=pltpu.PrefetchScalarGridSpec(
            num_scalar_prefetch=1,
            grid=(1,),
            in_specs=[pl.BlockSpec((rows, channels), lambda i, *_: (0, 0))] + [anywhere] * (len(pieces) + has_old),
            out_specs=anywhere,
            scratch_shapes=[
                pltpu.VMEM((len(blocks), width, channels), jnp.bfloat16),
                pltpu.VMEM((2, rows, width), jnp.bfloat16),
                pltpu.SemaphoreType.DMA((len(blocks), 4)),
                pltpu.SemaphoreType.DMA((len(blocks),)),
            ],
        ),
        input_output_aliases={2 + len(pieces): 0} if has_old else {},
        compiler_params=pltpu.CompilerParams(vmem_limit_bytes=VMEM_LIMIT),
        cost_estimate=pl.CostEstimate(
            flops=2 * rows * channels * width * len(blocks),
            bytes_accessed=2 * (channels * width + rows * width) * len(blocks) + 2 * rows * channels,
            transcendentals=0,
        ),
        name="project",
    )(scalars, att, *pieces, *([old] if has_old else []))


def on_device(groups, devices, queries, keys, values, counts, neighbours, gate_table, step, out_weight):
    slots, rows, channels = queries.shape
    shard = out_weight.shape[1]
    columns = shard * devices
    chips = devices // CORES
    length = chips // COLUMNS

    def permute(array, target):
        pairs = []
        for g in range(groups):
            for d in range(devices):
                to = target(g, d // (CORES * COLUMNS), d // CORES % COLUMNS, d % CORES)
                if to is not None:
                    tg, tz, tx, tc = to
                    pairs.append((g * devices + d, tg * devices + (tz * COLUMNS + tx) * CORES + tc))
        return lax.ppermute(array, ("groups", "dp"), pairs)

    def within_member(array, by):
        pairs = []
        for d in range(devices):
            first, second = (d, (d + by) % devices) if by > 0 else ((d + by) % devices, d)
            if (first - MEMBER_DEVS // 2) % MEMBER_DEVS != MEMBER_DEVS - 1:
                pairs.append((d, (d + by) % devices))
        return lax.ppermute(array, "dp", pairs)

    tail_start = jnp.maximum(counts[0] - HALO, 0)
    tail = jnp.stack([lax.dynamic_slice_in_dim(a, tail_start, HALO, 0) for a in (keys, values)])
    lead = jnp.stack([keys[:HALO], values[:HALO]])
    gate_row = lax.dynamic_slice_in_dim(gate_table, step[0], 1, 0)
    weight = out_weight.T

    if not (groups == 2 and devices % (CORES * COLUMNS) == 0 and length >= 3 and shard % 32 == 0 and (CORES * shard) % 128 == 0):
        before, after = within_member(tail, 1), within_member(lead, -1)
        att = attend(queries, keys, values, before, after, neighbours, counts, gate_row)
        full = lax.all_gather(weight, "dp", axis=0, tiled=True)
        mixed = lax.dot_general(
            att.reshape(slots * rows, channels), full, (((1,), (1,)), ((), ())), preferred_element_type=jnp.float32
        )
        return mixed.astype(jnp.bfloat16).reshape(slots, rows, columns)

    over = {
        "z": lambda g, z, x, c: (g, (z + 1) % length, x, c),
        "x": lambda g, z, x, c: (g, z, (x + 1) % COLUMNS, c),
        "y": lambda g, z, x, c: (1 - g, z, x, c),
        "s": lambda g, z, x, c: (g, z, x, 1 - c),
    }
    group = lax.axis_index("groups")
    device = lax.axis_index("dp")
    core = device % CORES
    my_x, my_z = device // CORES % COLUMNS, device // (CORES * COLUMNS)

    half = shard // 2
    have = {
        ("z", "p", 0): lax.dynamic_slice_in_dim(weight, group * half, half, 0),
        ("z", "q", 0): lax.dynamic_slice_in_dim(weight, (1 - group) * half, half, 0),
        "weight": weight,
    }
    sends = {
        "z": [(("z", "p", s), ("z", "p", s + 1)) for s in range(length - 1)]
        + [(("z", "q", s), ("z", "q", s + 1)) for s in range(1, length - 1)],
        "x": [(("z", "p", s), ("x", "p", s)) for s in range(length)] + [(("z", "q", 0), ("x", "q", 0))],
        "y": [None, (("z", "p", 1), ("z", "q", 1))] + [(("x", "p", s), ("x", "q", s)) for s in range(1, length)],
    }
    rounds = max(len(v) for v in sends.values())
    blocks = [("z", s) for s in range(length)] + [("x", s) for s in range(length)]
    todo = list(blocks)

    def ready():
        full = []
        for b in todo:
            if b == ("z", 0):
                ok = "s_weight" in have
            else:
                ok = all(("s", (b[0], h, b[1])) in have for h in "pq")
            if ok:
                full.append(b)
        return full

    def run_project(which, att, old):
        pieces, chip_of = [], []
        for b in which:
            col, s = b
            todo.remove(b)
            if b == ("z", 0):
                pieces.append([have["weight"], have["s_weight"]])
            else:
                mine = [(col, h, s) for h in "pq"]
                pieces.append([have[m] for m in mine] + [have[("s", m)] for m in mine])
            x = my_x if col == "z" else (my_x + 1) % COLUMNS
            chip_of.append((my_z - s) % length * COLUMNS + x)
        return project(att, pieces, chip_of, core, group, columns, old)

    att = out = None
    arrived = []
    swap = []
    for r in range(rounds + 1):
        names = list(arrived)
        keep = [have[n] for n in names]
        items = [(link, *sends[link][r]) for link in ("z", "x", "y") if r < len(sends[link]) and sends[link][r]]
        sources = [have[src] for _, src, _ in items]
        bar = lax.optimization_barrier((keep, sources, [a for a in (att, out) if a is not None], [have[n] for n in swap]))
        for n, a in zip(names, bar[0]):
            have[n] = a
        if att is not None:
            att = bar[2][0]
        if out is not None:
            out = bar[2][1]
        work = ready() if att is not None else []
        arrived = []
        for (link, _, dst), a in zip(items, bar[1]):
            have[dst] = permute(a, over[link])
            arrived.append(dst)
        if r == 0:
            have["before"], have["after"] = within_member(tail, 1), within_member(lead, -1)
        for n, a in zip(swap, bar[3]):
            to = "s_weight" if n == "weight" else ("s", n)
            have[to] = permute(a, over["s"])
            arrived.append(to)
        swap = [d for d in arrived if isinstance(d, tuple) and d[0] != "s"]
        if r == 0:
            swap.append("weight")
        if r == 1:
            arrived += ["before", "after"]
        if r == 2:
            att = attend(queries, keys, values, have["before"], have["after"], neighbours, counts, gate_row)
            att = att.reshape(slots * rows, channels)
        elif work:
            out = run_project(work, att, out)
    out = run_project(list(todo), att, out)
    return out.reshape(slots, rows, columns)


def solution(mesh):
    both = P(("groups", "dp"), None, None)
    placed = (both, both, both, P(("groups", "dp")), P(("groups", "dp"), None), P(), P(), P(None, "dp"))
    return jax.shard_map(
        functools.partial(on_device, mesh.shape["groups"], mesh.shape["dp"]),
        mesh=mesh,
        in_specs=placed,
        out_specs=both,
        check_vma=False,
    )
```

```python
import functools
import math

import jax
import jax.numpy as jnp
from jax import lax
from jax.experimental import pallas as pl
from jax.experimental.pallas import tpu as pltpu
from jax.sharding import PartitionSpec as P

HEADS = 20
HALO = 1
MEMBER_DEVS = 4
CORES = 2
COLUMNS = 2

masked_score = -1e30
HALO_ROUND = 1
VMEM_LIMIT = 60 * 1024 * 1024


def attention_kernel(first, index_ref, count_ref, q_hbm, k_hbm, v_hbm, before_hbm, after_hbm, gate_ref, o_ref, q_ref, ext_k, ext_v, sems):
    groups, slots, rows, width = q_ref.shape
    head_dim = q_hbm.shape[2] // HEADS
    places = slots + 2 * HALO
    picks = index_ref.shape[0] // slots
    to_exponent = math.log2(math.e) / math.sqrt(head_dim)

    def loads(g):
        at = pl.ds(pl.multiple_of((first + g) * width, width), width)
        pairs = [(q_hbm.at[:, :, at], q_ref.at[g])]
        for i, (own, ext) in enumerate(((k_hbm, ext_k), (v_hbm, ext_v))):
            pairs.append((before_hbm.at[i, :, :, at], ext.at[g, pl.ds(0, HALO)]))
            pairs.append((own.at[:, :, at], ext.at[g, pl.ds(HALO, slots)]))
            pairs.append((after_hbm.at[i, :, :, at], ext.at[g, pl.ds(HALO + slots, HALO)]))
        return [pltpu.make_async_copy(src, dst, sems.at[g, i]) for i, (src, dst) in enumerate(pairs)]

    for c in loads(0):
        c.start()

    def head_group(g, _):
        for c in loads(g):
            c.wait()

        @pl.when(g + 1 < groups)
        def _():
            for c in loads(g + 1):
                c.start()

        base = pl.multiple_of(g * width, width)
        for slot in range(slots):

            @pl.when(slot < count_ref[0])
            def _():
                place = [index_ref[slot * picks + j] for j in range(picks)]
                held = [jnp.minimum(p, places - 1) for p in place]
                ats = [pl.ds(h * head_dim, head_dim) for h in range(width // head_dim)]
                scored, weighed = [], []
                for at in ats:
                    query = q_ref[g, slot, :, at]
                    keyv = jnp.concatenate([ext_k[g, held[j], :, at] for j in range(picks)], axis=0)
                    scored.append(lax.dot_general(query, keyv, (((1,), (1,)), ((), ())), preferred_element_type=jnp.float32))
                for sc in scored:
                    sc = [jnp.where(place[j] < places, sc[:, j * rows : (j + 1) * rows], masked_score) for j in range(picks)]
                    top = jnp.max(functools.reduce(jnp.maximum, sc), axis=1, keepdims=True)
                    raw = [jnp.exp2((s - top) * to_exponent) for s in sc]
                    den = jnp.sum(functools.reduce(jnp.add, raw), axis=1, keepdims=True)
                    weighed.append((jnp.concatenate([r.astype(jnp.bfloat16) for r in raw], axis=1), den))
                for h, at in enumerate(ats):
                    out_at = pl.ds(pl.multiple_of(base + h * head_dim, head_dim), head_dim)
                    vals = jnp.concatenate([ext_v[g, held[j], :, at] for j in range(picks)], axis=0)
                    summed = jnp.dot(weighed[h][0], vals, preferred_element_type=jnp.float32)
                    o_ref[slot, :, out_at] = (summed * (1.0 / weighed[h][1]) * gate_ref[:, out_at]).astype(o_ref.dtype)

            @pl.when(slot >= count_ref[0])
            def _():
                o_ref[slot, :, pl.ds(base, width)] = jnp.zeros((rows, width), o_ref.dtype)

        return 0

    lax.fori_loop(0, groups, head_group, 0)


def attend(queries, keys, values, before, after, neighbours, counts, gate_row, part=0, parts=1):
    slots, rows, channels = queries.shape
    head_dim = channels // HEADS
    heads = 4 if HEADS % 4 == 0 else 1
    width = heads * head_dim
    places = slots + 2 * HALO
    first, last = (-(-(HEADS // heads) * p // parts) for p in (part, part + 1))
    groups = last - first
    gate_row = gate_row[:, first * width : last * width]
    hbm = pl.BlockSpec(memory_space=pltpu.HBM)
    pairs = slots * groups * heads * rows * (neighbours.shape[0] // slots) * rows
    return pl.pallas_call(
        functools.partial(attention_kernel, first),
        out_shape=jax.ShapeDtypeStruct((slots, rows, groups * width), jnp.bfloat16),
        grid_spec=pltpu.PrefetchScalarGridSpec(
            num_scalar_prefetch=2,
            grid=(1,),
            in_specs=[hbm] * 5 + [pl.BlockSpec((1, groups * width), lambda i, *_: (0, 0))],
            out_specs=pl.BlockSpec((slots, rows, groups * width), lambda i, *_: (0, 0, 0)),
            scratch_shapes=[
                pltpu.VMEM((groups, slots, rows, width), jnp.bfloat16),
                pltpu.VMEM((groups, places, rows, width), jnp.bfloat16),
                pltpu.VMEM((groups, places, rows, width), jnp.bfloat16),
                pltpu.SemaphoreType.DMA((groups, 7)),
            ],
        ),
        compiler_params=pltpu.CompilerParams(vmem_limit_bytes=VMEM_LIMIT),
        cost_estimate=pl.CostEstimate(
            flops=4 * pairs * head_dim, bytes_accessed=12 * slots * rows * groups * width, transcendentals=pairs
        ),
        name="attention",
    )(neighbours, counts, queries, keys, values, before, after, gate_row)


def project_kernel(pieces_of, group_ref, own_hbm, sibling_hbm, *refs):
    n = sum(pieces_of)
    own_ref, sibling_ref, att_ref, wbuf, att_sem, in_sem = refs[n:]
    rows = own_hbm.shape[0]
    group = group_ref[0]
    begins, loads, at = [], [], 0
    for b, count in enumerate(pieces_of):
        begins.append(at)
        copies = []
        first = sum(pieces_of[:b])
        for i, piece in enumerate(refs[first : first + count]):
            high = piece.shape[0]
            start = begins[-1]
            if count == 2:
                start = start + (group if i == 0 else 1 - group) * high
            start = pl.multiple_of(start, high)
            copies.append(pltpu.make_async_copy(piece, wbuf.at[pl.ds(start, high)], in_sem.at[b, i]))
            at += high
        loads.append(copies)
    att_loads = [
        pltpu.make_async_copy(src, att_ref.at[pl.ds(i * rows, rows)], att_sem.at[i])
        for i, src in enumerate((own_hbm, sibling_hbm))
    ]
    for c in loads[0] + att_loads:
        c.start()
    asked, arrived, done = 1, 0, 0
    while done < at:
        step = min(256, at - done)
        while arrived < len(loads) and begins[arrived] < done + step:
            for c in loads[arrived]:
                c.wait()
            arrived += 1
            if asked < len(loads):
                for c in loads[asked]:
                    c.start()
                asked += 1
        if done == 0:
            for c in att_loads:
                c.wait()
        for i, ref in enumerate((own_ref, sibling_ref)):
            ref[:, done : done + step] = lax.dot_general(
                att_ref[i * rows : (i + 1) * rows],
                wbuf[done : done + step],
                (((1,), (1,)), ((), ())),
                preferred_element_type=jnp.float32,
            ).astype(ref.dtype)
        done += step


def project(own, sibling, blocks, group):
    rows, channels = own.shape
    pieces = [p for b in blocks for p in b]
    width = sum(p.shape[0] for p in pieces)
    padded = -(-width // 128) * 128
    hbm = pl.BlockSpec(memory_space=pltpu.HBM)
    result = jax.ShapeDtypeStruct((rows, padded), jnp.bfloat16)
    return pl.pallas_call(
        functools.partial(project_kernel, tuple(len(b) for b in blocks)),
        out_shape=(result, result),
        grid_spec=pltpu.PrefetchScalarGridSpec(
            num_scalar_prefetch=1,
            grid=(1,),
            in_specs=[hbm] * (2 + len(pieces)),
            out_specs=(pl.BlockSpec((rows, padded), lambda i, *_: (0, 0)),) * 2,
            scratch_shapes=[
                pltpu.VMEM((2 * rows, channels), jnp.bfloat16),
                pltpu.VMEM((width, channels), jnp.bfloat16),
                pltpu.SemaphoreType.DMA((2,)),
                pltpu.SemaphoreType.DMA((len(blocks), 2)),
            ],
        ),
        compiler_params=pltpu.CompilerParams(vmem_limit_bytes=VMEM_LIMIT),
        cost_estimate=pl.CostEstimate(
            flops=4 * rows * channels * width,
            bytes_accessed=2 * (channels * width + 2 * rows * (channels + width)),
            transcendentals=0,
        ),
        name="project",
    )(group.reshape(1), own, sibling, *pieces)


def assemble_kernel(places, shard, has_old, scalars, *refs):
    arrays, (out_ref, buf, sem) = refs[: len(refs) - 3 - has_old], refs[-3:]
    half = shard // 2
    stores = []
    for b, parts in enumerate(places):
        if b >= 2:
            stores[b - 2].wait()

        def place(first_core, group):
            for c in range(CORES):
                for i, (array, lane) in enumerate(parts):
                    src = arrays[2 * array + (0 if c == first_core else 1)]
                    high = shard if len(parts) == 1 else half
                    to = c * shard + (0 if len(parts) == 1 else (group if i == 0 else 1 - group) * half)
                    buf[b % 2, :, to : to + high] = src[:, lane : lane + high]

        if len(parts) == 1:
            for c in range(CORES):
                pl.when(scalars[0] == c)(functools.partial(place, c, 0))
        else:
            for c in range(CORES):
                for g in range(2):
                    pl.when((scalars[0] == c) & (scalars[1] == g))(functools.partial(place, c, g))
        where = pl.ds(pl.multiple_of(scalars[2 + b] * CORES * shard, CORES * shard), CORES * shard)
        store = pltpu.make_async_copy(buf.at[b % 2], out_ref.at[:, where], sem.at[b % 2])
        store.start()
        stores.append(store)
    for store in stores[-2:]:
        store.wait()


def assemble(arrays, places, scalars, shard, columns, old=None):
    rows = arrays[0].shape[0]
    has_old = int(old is not None)
    hbm = pl.BlockSpec(memory_space=pltpu.HBM)
    return pl.pallas_call(
        functools.partial(assemble_kernel, places, shard, has_old),
        out_shape=jax.ShapeDtypeStruct((rows, columns), jnp.bfloat16),
        grid_spec=pltpu.PrefetchScalarGridSpec(
            num_scalar_prefetch=1,
            grid=(1,),
            in_specs=[pl.BlockSpec(a.shape, lambda i, *_: (0, 0)) for a in arrays] + [hbm] * has_old,
            out_specs=hbm,
            scratch_shapes=[pltpu.VMEM((2, rows, CORES * shard), jnp.bfloat16), pltpu.SemaphoreType.DMA((2,))],
        ),
        input_output_aliases={1 + len(arrays): 0} if has_old else {},
        compiler_params=pltpu.CompilerParams(vmem_limit_bytes=VMEM_LIMIT),
        cost_estimate=pl.CostEstimate(
            flops=0, bytes_accessed=4 * rows * (CORES * shard * len(places)), transcendentals=0
        ),
        name="assemble",
    )(scalars, *arrays, *([old] if has_old else []))


def on_device(groups, devices, queries, keys, values, counts, neighbours, gate_table, step, out_weight):
    slots, rows, channels = queries.shape
    shard = out_weight.shape[1]
    columns = shard * devices
    chips = devices // CORES
    length = chips // COLUMNS

    def permute(array, target):
        pairs = []
        for g in range(groups):
            for d in range(devices):
                to = target(g, d // (CORES * COLUMNS), d // CORES % COLUMNS, d % CORES)
                if to is not None:
                    tg, tz, tx, tc = to
                    pairs.append((g * devices + d, tg * devices + (tz * COLUMNS + tx) * CORES + tc))
        return lax.ppermute(array, ("groups", "dp"), pairs)

    def within_member(array, by):
        pairs = []
        for d in range(devices):
            first, second = (d, (d + by) % devices) if by > 0 else ((d + by) % devices, d)
            if (first - MEMBER_DEVS // 2) % MEMBER_DEVS != MEMBER_DEVS - 1:
                pairs.append((d, (d + by) % devices))
        return lax.ppermute(array, "dp", pairs)

    tail_start = jnp.maximum(counts[0] - HALO, 0)
    tail = jnp.stack([lax.dynamic_slice_in_dim(a, tail_start, HALO, 0) for a in (keys, values)])
    lead = jnp.stack([keys[:HALO], values[:HALO]])
    gate_row = lax.dynamic_slice_in_dim(gate_table, step[0], 1, 0)
    weight = out_weight.T

    if not (groups == 2 and devices % (CORES * COLUMNS) == 0 and length >= 3 and shard % 32 == 0 and (CORES * shard) % 128 == 0):
        before, after = within_member(tail, 1), within_member(lead, -1)
        att = attend(queries, keys, values, before, after, neighbours.reshape(-1), counts, gate_row)
        full = lax.all_gather(weight, "dp", axis=0, tiled=True)
        mixed = lax.dot_general(
            att.reshape(slots * rows, channels), full, (((1,), (1,)), ((), ())), preferred_element_type=jnp.float32
        )
        return mixed.astype(jnp.bfloat16).reshape(slots, rows, columns)

    over = {
        "z": lambda g, z, x, c: (g, (z + 1) % length, x, c),
        "x": lambda g, z, x, c: (g, z, (x + 1) % COLUMNS, c),
        "y": lambda g, z, x, c: (1 - g, z, x, c),
        "s": lambda g, z, x, c: (g, z, x, 1 - c),
    }
    group = lax.axis_index("groups")
    device = lax.axis_index("dp")
    core = device % CORES
    my_x, my_z = device // CORES % COLUMNS, device // (CORES * COLUMNS)

    half = shard // 2
    have = {
        ("z", "p", 0): lax.dynamic_slice_in_dim(weight, group * half, half, 0),
        "weight": weight,
    }
    sends = {
        "z": [(("z", "p", s), ("z", "p", s + 1)) for s in range(length - 1)]
        + [(("z", "q", s), ("z", "q", s + 1)) for s in range(1, length - 1)],
        "x": [(("z", "p", s), ("x", "p", s)) for s in range(length)] + [(("z", "q", 0), ("x", "q", 0))],
        "y": [None, (("z", "p", 1), ("z", "q", 1))] + [(("x", "p", s), ("x", "q", s)) for s in range(1, length)],
    }
    rounds = max(len(v) for v in sends.values())
    every = [("z", s) for s in range(length)] + [("x", s) for s in range(length)]

    def names_of(b):
        return ["weight"] if b == ("z", 0) else [(b[0], h, b[1]) for h in "pq"]

    def chip_of(b):
        x = my_x if b[0] == "z" else (my_x + 1) % COLUMNS
        return (my_z - b[1]) % length * COLUMNS + x

    by_then = {"weight", ("z", "p", 0)} | {s[1] for link in sends.values() for s in link[: rounds - 1] if s}
    whole = [b for b in every if all(n in by_then for n in names_of(b))]
    halves = [b for b in every if b not in whole]
    scalars = [jnp.stack([core, group] + [chip_of(b) for b in bs]).astype(jnp.int32) for bs in (whole, halves)]
    small = [neighbours.reshape(-1), gate_row, scalars, group.reshape(1)]

    arrived, att, att_sibling, early = [], None, None, None
    for r in range(rounds):
        names = list(arrived)
        items = [(link, *sends[link][r]) for link in ("z", "x", "y") if r < len(sends[link]) and sends[link][r]]
        halo = [tail, lead] if r == HALO_ROUND else []
        if r == rounds - 1:
            have[("z", "q", 0)] = weight
        bar = lax.optimization_barrier(
            ([have[n] for n in names], [have[src] for _, src, _ in items], att, att_sibling, halo, small if r else [])
        )
        for n, a in zip(names, bar[0]):
            have[n] = a
        _, sources, att, att_sibling, halo, small = (*bar[:5], bar[5] if r else small)
        arrived = []
        for (link, src, dst), a in zip(items, sources):
            if src == ("z", "q", 0):
                a = lax.dynamic_slice_in_dim(a, (1 - group) * half, half, 0)
            have[dst] = permute(a, over[link])
            arrived.append(dst)
        if halo:
            have["before"], have["after"] = within_member(halo[0], 1), within_member(halo[1], -1)
            arrived += ["before", "after"]
        if r == HALO_ROUND + 1:
            att = attend(queries, keys, values, have["before"], have["after"], small[0], counts, small[1])
            att = att.reshape(slots * rows, channels)
        elif r == HALO_ROUND + 2:
            att_sibling = permute(att, over["s"])
        if r == rounds - 1:
            pieces = [[have[n] for n in names_of(b)] for b in whole] + [[have[(b[0], "p", b[1])]] for b in halves]
            early = project(att, att_sibling, pieces, small[3])
    names = list(arrived)
    bar, early, att, att_sibling = lax.optimization_barrier(([have[n] for n in names], early, att, att_sibling))
    for n, a in zip(names, bar):
        have[n] = a
    early = [early[0], permute(early[1], over["s"])]
    late = project(att, att_sibling, [[have[(b[0], "q", b[1])]] for b in halves], small[3])
    late = [late[0], permute(late[1], over["s"])]
    out = assemble(early, tuple(((0, i * shard),) for i in range(len(whole))), small[2][0], shard, columns)
    at = len(whole) * shard
    places = tuple(((0, at + i * half), (1, i * half)) for i in range(len(halves)))
    out = assemble(early + late, places, small[2][1], shard, columns, out)
    return out.reshape(slots, rows, columns)


def solution(mesh):
    both = P(("groups", "dp"), None, None)
    placed = (both, both, both, P(("groups", "dp")), P(("groups", "dp"), None), P(), P(), P(None, "dp"))
    return jax.shard_map(
        functools.partial(on_device, mesh.shape["groups"], mesh.shape["dp"]),
        mesh=mesh,
        in_specs=placed,
        out_specs=both,
        check_vma=False,
    )
```

```python
import functools
import math

import jax
import jax.numpy as jnp
from jax import lax
from jax.experimental import pallas as pl
from jax.experimental.pallas import tpu as pltpu
from jax.sharding import PartitionSpec as P

HEADS = 20
HALO = 1
MEMBER_DEVS = 4
CORES = 2
COLUMNS = 2

masked_score = -1e30
HALO_ROUND = 1
VMEM_LIMIT = 60 * 1024 * 1024


def attention_kernel(first, index_ref, count_ref, q_hbm, k_hbm, v_hbm, before_hbm, after_hbm, gate_ref, o_ref, q_ref, ext_k, ext_v, sems):
    groups, slots, rows, width = q_ref.shape
    head_dim = q_hbm.shape[2] // HEADS
    places = slots + 2 * HALO
    picks = index_ref.shape[0] // slots
    to_exponent = math.log2(math.e) / math.sqrt(head_dim)

    def loads(g):
        at = pl.ds(pl.multiple_of((first + g) * width, width), width)
        pairs = [(q_hbm.at[:, :, at], q_ref.at[g])]
        for i, (own, ext) in enumerate(((k_hbm, ext_k), (v_hbm, ext_v))):
            pairs.append((before_hbm.at[i, :, :, at], ext.at[g, pl.ds(0, HALO)]))
            pairs.append((own.at[:, :, at], ext.at[g, pl.ds(HALO, slots)]))
            pairs.append((after_hbm.at[i, :, :, at], ext.at[g, pl.ds(HALO + slots, HALO)]))
        return [pltpu.make_async_copy(src, dst, sems.at[g, i]) for i, (src, dst) in enumerate(pairs)]

    for c in loads(0):
        c.start()

    def head_group(g, _):
        for c in loads(g):
            c.wait()

        @pl.when(g + 1 < groups)
        def _():
            for c in loads(g + 1):
                c.start()

        base = pl.multiple_of(g * width, width)
        for slot in range(slots):

            @pl.when(slot < count_ref[0])
            def _():
                place = [index_ref[slot * picks + j] for j in range(picks)]
                held = [jnp.minimum(p, places - 1) for p in place]
                ats = [pl.ds(h * head_dim, head_dim) for h in range(width // head_dim)]
                scored, weighed = [], []
                for at in ats:
                    query = q_ref[g, slot, :, at]
                    keyv = jnp.concatenate([ext_k[g, held[j], :, at] for j in range(picks)], axis=0)
                    scored.append(lax.dot_general(query, keyv, (((1,), (1,)), ((), ())), preferred_element_type=jnp.float32))
                for sc in scored:
                    sc = [jnp.where(place[j] < places, sc[:, j * rows : (j + 1) * rows], masked_score) for j in range(picks)]
                    top = jnp.max(functools.reduce(jnp.maximum, sc), axis=1, keepdims=True)
                    raw = [jnp.exp2((s - top) * to_exponent) for s in sc]
                    den = jnp.sum(functools.reduce(jnp.add, raw), axis=1, keepdims=True)
                    weighed.append((jnp.concatenate([r.astype(jnp.bfloat16) for r in raw], axis=1), den))
                for h, at in enumerate(ats):
                    out_at = pl.ds(pl.multiple_of(base + h * head_dim, head_dim), head_dim)
                    vals = jnp.concatenate([ext_v[g, held[j], :, at] for j in range(picks)], axis=0)
                    summed = jnp.dot(weighed[h][0], vals, preferred_element_type=jnp.float32)
                    o_ref[slot, :, out_at] = (summed * (1.0 / weighed[h][1]) * gate_ref[:, out_at]).astype(o_ref.dtype)

            @pl.when(slot >= count_ref[0])
            def _():
                o_ref[slot, :, pl.ds(base, width)] = jnp.zeros((rows, width), o_ref.dtype)

        return 0

    lax.fori_loop(0, groups, head_group, 0)


def attend(queries, keys, values, halo, neighbours, counts, gate_row, part=0, parts=1):
    slots, rows, channels = queries.shape
    head_dim = channels // HEADS
    heads = 4 if HEADS % 4 == 0 else 1
    width = heads * head_dim
    places = slots + 2 * HALO
    first, last = (-(-(HEADS // heads) * p // parts) for p in (part, part + 1))
    groups = last - first
    gate_row = gate_row[:, first * width : last * width]
    hbm = pl.BlockSpec(memory_space=pltpu.HBM)
    pairs = slots * groups * heads * rows * (neighbours.shape[0] // slots) * rows
    return pl.pallas_call(
        functools.partial(attention_kernel, first),
        out_shape=jax.ShapeDtypeStruct((slots, rows, groups * width), jnp.bfloat16),
        grid_spec=pltpu.PrefetchScalarGridSpec(
            num_scalar_prefetch=2,
            grid=(1,),
            in_specs=[hbm] * 5 + [pl.BlockSpec((1, groups * width), lambda i, *_: (0, 0))],
            out_specs=pl.BlockSpec((slots, rows, groups * width), lambda i, *_: (0, 0, 0)),
            scratch_shapes=[
                pltpu.VMEM((groups, slots, rows, width), jnp.bfloat16),
                pltpu.VMEM((groups, places, rows, width), jnp.bfloat16),
                pltpu.VMEM((groups, places, rows, width), jnp.bfloat16),
                pltpu.SemaphoreType.DMA((groups, 7)),
            ],
        ),
        compiler_params=pltpu.CompilerParams(vmem_limit_bytes=VMEM_LIMIT),
        cost_estimate=pl.CostEstimate(
            flops=4 * pairs * head_dim, bytes_accessed=12 * slots * rows * groups * width, transcendentals=pairs
        ),
        name="attention",
    )(neighbours, counts, queries, keys, values, *halo, gate_row)


def project_kernel(pieces_of, group_ref, own_hbm, sibling_hbm, *refs):
    n = sum(pieces_of)
    own_ref, sibling_ref, att_ref, wbuf, att_sem, in_sem = refs[n:]
    rows = own_hbm.shape[0]
    group = group_ref[0]
    begins, loads, at = [], [], 0
    for b, count in enumerate(pieces_of):
        begins.append(at)
        copies = []
        first = sum(pieces_of[:b])
        for i, piece in enumerate(refs[first : first + count]):
            high = piece.shape[0]
            start = begins[-1]
            if count == 2:
                start = start + (group if i == 0 else 1 - group) * high
            start = pl.multiple_of(start, high)
            copies.append(pltpu.make_async_copy(piece, wbuf.at[pl.ds(start, high)], in_sem.at[b, i]))
            at += high
        loads.append(copies)
    att_loads = [
        pltpu.make_async_copy(src, att_ref.at[pl.ds(i * rows, rows)], att_sem.at[i])
        for i, src in enumerate((own_hbm, sibling_hbm))
    ]
    for c in att_loads[:1] + loads[0] + att_loads[1:]:
        c.start()
    asked, arrived, done = 1, 0, 0
    while done < at:
        step = min(256, at - done)
        while arrived < len(loads) and begins[arrived] < done + step:
            for c in loads[arrived]:
                c.wait()
            arrived += 1
            if asked < len(loads):
                for c in loads[asked]:
                    c.start()
                asked += 1
        for i, ref in enumerate((own_ref, sibling_ref)):
            if done == 0:
                att_loads[i].wait()
            ref[:, done : done + step] = lax.dot_general(
                att_ref[i * rows : (i + 1) * rows],
                wbuf[done : done + step],
                (((1,), (1,)), ((), ())),
                preferred_element_type=jnp.float32,
            ).astype(ref.dtype)
        done += step


def project(own, sibling, blocks, group):
    rows, channels = own.shape
    pieces = [p for b in blocks for p in b]
    width = sum(p.shape[0] for p in pieces)
    padded = -(-width // 128) * 128
    hbm = pl.BlockSpec(memory_space=pl.ANY)
    limit = (32 if len(pieces) > 4 else 20) * 1024 * 1024
    result = jax.ShapeDtypeStruct((rows, padded), jnp.bfloat16)
    return pl.pallas_call(
        functools.partial(project_kernel, tuple(len(b) for b in blocks)),
        out_shape=(result, result),
        grid_spec=pltpu.PrefetchScalarGridSpec(
            num_scalar_prefetch=1,
            grid=(1,),
            in_specs=[hbm] * (2 + len(pieces)),
            out_specs=(pl.BlockSpec((rows, padded), lambda i, *_: (0, 0)),) * 2,
            scratch_shapes=[
                pltpu.VMEM((2 * rows, channels), jnp.bfloat16),
                pltpu.VMEM((width, channels), jnp.bfloat16),
                pltpu.SemaphoreType.DMA((2,)),
                pltpu.SemaphoreType.DMA((len(blocks), 2)),
            ],
        ),
        compiler_params=pltpu.CompilerParams(vmem_limit_bytes=limit),
        cost_estimate=pl.CostEstimate(
            flops=4 * rows * channels * width,
            bytes_accessed=2 * (channels * width + 2 * rows * (channels + width)),
            transcendentals=0,
        ),
        name="project",
    )(group.reshape(1), own, sibling, *pieces)


def assemble_kernel(places, shard, scalars, *refs):
    arrays, (out_ref, buf, sem) = refs[:-3], refs[-3:]
    half = shard // 2
    high = buf.shape[1]
    rows = pl.ds(pl.multiple_of(pl.program_id(0) * high, high), high)
    stores = []
    for b, parts in enumerate(places):

        def place(first_core, group):
            for c in range(CORES):
                for i, (array, lane) in enumerate(parts):
                    src = arrays[2 * array + (0 if c == first_core else 1)]
                    wide = shard if len(parts) == 1 else half
                    to = c * shard + (0 if len(parts) == 1 else (group if i == 0 else 1 - group) * half)
                    buf[b, :, to : to + wide] = src[:, lane : lane + wide]

        if len(parts) == 1:
            for c in range(CORES):
                pl.when(scalars[0] == c)(functools.partial(place, c, 0))
        else:
            for c in range(CORES):
                for g in range(2):
                    pl.when((scalars[0] == c) & (scalars[1] == g))(functools.partial(place, c, g))
        where = pl.ds(pl.multiple_of(scalars[2 + b] * CORES * shard, CORES * shard), CORES * shard)
        store = pltpu.make_async_copy(buf.at[b], out_ref.at[rows, where], sem.at[b])
        store.start()
        stores.append(store)
    for store in stores:
        store.wait()


def assemble(arrays, places, scalars, shard, columns):
    rows = arrays[0].shape[0]
    chunk = 128 if rows % 128 == 0 else rows
    return pl.pallas_call(
        functools.partial(assemble_kernel, places, shard),
        out_shape=jax.ShapeDtypeStruct((rows, columns), jnp.bfloat16),
        grid_spec=pltpu.PrefetchScalarGridSpec(
            num_scalar_prefetch=1,
            grid=(rows // chunk,),
            in_specs=[pl.BlockSpec((chunk, a.shape[1]), lambda i, *_: (i, 0)) for a in arrays],
            out_specs=pl.BlockSpec(memory_space=pltpu.HBM),
            scratch_shapes=[
                pltpu.VMEM((len(places), chunk, CORES * shard), jnp.bfloat16),
                pltpu.SemaphoreType.DMA((len(places),)),
            ],
        ),
        compiler_params=pltpu.CompilerParams(vmem_limit_bytes=20 * 1024 * 1024),
        cost_estimate=pl.CostEstimate(flops=0, bytes_accessed=4 * rows * columns, transcendentals=0),
        name="assemble",
    )(scalars, *arrays)


def on_device(groups, devices, queries, keys, values, counts, neighbours, gate_table, step, out_weight):
    slots, rows, channels = queries.shape
    shard = out_weight.shape[1]
    columns = shard * devices
    chips = devices // CORES
    length = chips // COLUMNS

    def permute(array, target):
        pairs = []
        for g in range(groups):
            for d in range(devices):
                to = target(g, d // (CORES * COLUMNS), d // CORES % COLUMNS, d % CORES)
                if to is not None:
                    tg, tz, tx, tc = to
                    pairs.append((g * devices + d, tg * devices + (tz * COLUMNS + tx) * CORES + tc))
        return lax.ppermute(array, ("groups", "dp"), pairs)

    def within_member(array, by):
        pairs = []
        for d in range(devices):
            first, second = (d, (d + by) % devices) if by > 0 else ((d + by) % devices, d)
            if (first - MEMBER_DEVS // 2) % MEMBER_DEVS != MEMBER_DEVS - 1:
                pairs.append((d, (d + by) % devices))
        return lax.ppermute(array, "dp", pairs)

    tail_start = jnp.maximum(counts[0] - HALO, 0)
    edges = [(lax.dynamic_slice_in_dim(a, tail_start, HALO, 0), a[:HALO]) for a in (keys, values)]
    gate_row = lax.dynamic_slice_in_dim(gate_table, step[0], 1, 0)
    weight = out_weight.T

    if not (groups == 2 and devices % (CORES * COLUMNS) == 0 and length >= 3 and shard % 32 == 0 and (CORES * shard) % 128 == 0):
        halo = [within_member(jnp.stack(e), by) for e, by in zip(zip(*edges), (1, -1))]
        att = attend(queries, keys, values, halo, neighbours.reshape(-1), counts, gate_row)
        full = lax.all_gather(weight, "dp", axis=0, tiled=True)
        mixed = lax.dot_general(
            att.reshape(slots * rows, channels), full, (((1,), (1,)), ((), ())), preferred_element_type=jnp.float32
        )
        return mixed.astype(jnp.bfloat16).reshape(slots, rows, columns)

    over = {
        "z": lambda g, z, x, c: (g, (z + 1) % length, x, c),
        "x": lambda g, z, x, c: (g, z, (x + 1) % COLUMNS, c),
        "y": lambda g, z, x, c: (1 - g, z, x, c),
        "s": lambda g, z, x, c: (g, z, x, 1 - c),
    }
    group = lax.axis_index("groups")
    device = lax.axis_index("dp")
    core = device % CORES
    my_x, my_z = device // CORES % COLUMNS, device // (CORES * COLUMNS)

    half = shard // 2
    have = {
        ("z", "p", 0): lax.dynamic_slice_in_dim(weight, group * half, half, 0),
        "weight": weight,
    }
    sends = {
        "z": [(("z", "p", s), ("z", "p", s + 1)) for s in range(length - 1)]
        + [(("z", "q", s), ("z", "q", s + 1)) for s in range(1, length - 1)],
        "x": [(("z", "p", s), ("x", "p", s)) for s in range(length)] + [(("z", "q", 0), ("x", "q", 0))],
        "y": [None, (("z", "p", 1), ("z", "q", 1))] + [(("x", "p", s), ("x", "q", s)) for s in range(1, length)],
    }
    rounds = max(len(v) for v in sends.values())
    every = [("z", s) for s in range(length)] + [("x", s) for s in range(length)]

    def names_of(b):
        return ["weight"] if b == ("z", 0) else [(b[0], h, b[1]) for h in "pq"]

    def chip_of(b):
        x = my_x if b[0] == "z" else (my_x + 1) % COLUMNS
        return (my_z - b[1]) % length * COLUMNS + x

    by_then = {"weight", ("z", "p", 0)} | {s[1] for link in sends.values() for s in link[: rounds - 1] if s}
    whole = [b for b in every if all(n in by_then for n in names_of(b))]
    halves = [b for b in every if b not in whole]
    scalars = jnp.stack([core, group] + [chip_of(b) for b in whole + halves]).astype(jnp.int32)
    small = [neighbours.reshape(-1), gate_row, scalars, group.reshape(1), weight]

    arrived, att, att_sibling, early = [], None, None, None
    for r in range(rounds):
        names = list(arrived)
        items = [(link, *sends[link][r]) for link in ("z", "x", "y") if r < len(sends[link]) and sends[link][r]]
        edge = [jnp.stack(e) for e in zip(*edges)] if r == HALO_ROUND else []
        bar = lax.optimization_barrier(
            ([have[n] for n in names], [have[src] for _, src, _ in items], att, att_sibling, edge, small if r else [])
        )
        for n, a in zip(names, bar[0]):
            have[n] = a
        _, sources, att, att_sibling, edge, small = (*bar[:5], bar[5] if r else small)
        arrived = []
        for (link, src, dst), a in zip(items, sources):
            have[dst] = permute(a, over[link])
            arrived.append(dst)
        for by, a in zip((1, -1), edge):
            have["halo", by] = within_member(a, by)
        if r == 1:
            have[("z", "q", 0)] = lax.dynamic_slice_in_dim(small[4], (1 - group) * half, half, 0)
            arrived.append(("z", "q", 0))
        if r == HALO_ROUND + 1:
            halo = [have["halo", by] for by in (1, -1)]
            att = attend(queries, keys, values, halo, small[0], counts, small[1])
            att = att.reshape(slots * rows, channels)
        elif r == HALO_ROUND + 2:
            att_sibling = permute(att, over["s"])
        if r == rounds - 1:
            pieces = [[have[n] for n in names_of(b)] for b in whole] + [[have[(b[0], "p", b[1])]] for b in halves]
            early = project(att, att_sibling, pieces, small[3])
    names = list(arrived)
    bar, early, att, att_sibling = lax.optimization_barrier(([have[n] for n in names], early, att, att_sibling))
    for n, a in zip(names, bar):
        have[n] = a
    early = [early[0], permute(early[1], over["s"])]
    late = project(att, att_sibling, [[have[(b[0], "q", b[1])]] for b in halves], small[3])
    late = [late[0], permute(late[1], over["s"])]
    at = len(whole) * shard
    places = tuple(((0, i * shard),) for i in range(len(whole)))
    places += tuple(((0, at + i * half), (1, i * half)) for i in range(len(halves)))
    out = assemble(early + late, places, small[2], shard, columns)
    return out.reshape(slots, rows, columns)


def solution(mesh):
    both = P(("groups", "dp"), None, None)
    placed = (both, both, both, P(("groups", "dp")), P(("groups", "dp"), None), P(), P(), P(None, "dp"))
    return jax.shard_map(
        functools.partial(on_device, mesh.shape["groups"], mesh.shape["dp"]),
        mesh=mesh,
        in_specs=placed,
        out_specs=both,
        check_vma=False,
    )
```

```python
import functools
import math

import jax
import jax.numpy as jnp
from jax import lax
from jax.experimental import pallas as pl
from jax.experimental.pallas import tpu as pltpu
from jax.sharding import PartitionSpec as P

HEADS = 20
HALO = 1
MEMBER_DEVS = 4
CORES = 2
COLUMNS = 2

masked_score = -1e30
HALO_ROUND = 1
VMEM_LIMIT = 60 * 1024 * 1024


def attention_kernel(first, index_ref, count_ref, q_hbm, k_hbm, v_hbm, before_hbm, after_hbm, gate_ref, o_ref, q_ref, ext_k, ext_v, sems):
    groups, slots, rows, width = q_ref.shape
    head_dim = q_hbm.shape[2] // HEADS
    places = slots + 2 * HALO
    picks = index_ref.shape[0] // slots
    to_exponent = math.log2(math.e) / math.sqrt(head_dim)

    def loads(g):
        at = pl.ds(pl.multiple_of((first + g) * width, width), width)
        pairs = [(q_hbm.at[:, :, at], q_ref.at[g])]
        for i, (own, ext) in enumerate(((k_hbm, ext_k), (v_hbm, ext_v))):
            pairs.append((before_hbm.at[i, :, :, at], ext.at[g, pl.ds(0, HALO)]))
            pairs.append((own.at[:, :, at], ext.at[g, pl.ds(HALO, slots)]))
            pairs.append((after_hbm.at[i, :, :, at], ext.at[g, pl.ds(HALO + slots, HALO)]))
        return [pltpu.make_async_copy(src, dst, sems.at[g, i]) for i, (src, dst) in enumerate(pairs)]

    for c in loads(0):
        c.start()

    def head_group(g, _):
        for c in loads(g):
            c.wait()

        @pl.when(g + 1 < groups)
        def _():
            for c in loads(g + 1):
                c.start()

        base = pl.multiple_of(g * width, width)
        for slot in range(slots):

            @pl.when(slot < count_ref[0])
            def _():
                place = [index_ref[slot * picks + j] for j in range(picks)]
                held = [jnp.minimum(p, places - 1) for p in place]
                ats = [pl.ds(h * head_dim, head_dim) for h in range(width // head_dim)]
                scored, weighed = [], []
                for at in ats:
                    query = q_ref[g, slot, :, at]
                    keyv = jnp.concatenate([ext_k[g, held[j], :, at] for j in range(picks)], axis=0)
                    scored.append(lax.dot_general(query, keyv, (((1,), (1,)), ((), ())), preferred_element_type=jnp.float32))
                for sc in scored:
                    sc = [jnp.where(place[j] < places, sc[:, j * rows : (j + 1) * rows], masked_score) for j in range(picks)]
                    top = jnp.max(functools.reduce(jnp.maximum, sc), axis=1, keepdims=True)
                    raw = [jnp.exp2((s - top) * to_exponent) for s in sc]
                    den = jnp.sum(functools.reduce(jnp.add, raw), axis=1, keepdims=True)
                    weighed.append((jnp.concatenate([r.astype(jnp.bfloat16) for r in raw], axis=1), den))
                for h, at in enumerate(ats):
                    out_at = pl.ds(pl.multiple_of(base + h * head_dim, head_dim), head_dim)
                    vals = jnp.concatenate([ext_v[g, held[j], :, at] for j in range(picks)], axis=0)
                    summed = jnp.dot(weighed[h][0], vals, preferred_element_type=jnp.float32)
                    o_ref[slot, :, out_at] = (summed * (1.0 / weighed[h][1]) * gate_ref[:, out_at]).astype(o_ref.dtype)

            @pl.when(slot >= count_ref[0])
            def _():
                o_ref[slot, :, pl.ds(base, width)] = jnp.zeros((rows, width), o_ref.dtype)

        return 0

    lax.fori_loop(0, groups, head_group, 0)


def attend(queries, keys, values, halo, neighbours, counts, gate_row, part=0, parts=1):
    slots, rows, channels = queries.shape
    head_dim = channels // HEADS
    heads = 4 if HEADS % 4 == 0 else 1
    width = heads * head_dim
    places = slots + 2 * HALO
    first, last = (-(-(HEADS // heads) * p // parts) for p in (part, part + 1))
    groups = last - first
    gate_row = gate_row[:, first * width : last * width]
    hbm = pl.BlockSpec(memory_space=pltpu.HBM)
    pairs = slots * groups * heads * rows * (neighbours.shape[0] // slots) * rows
    return pl.pallas_call(
        functools.partial(attention_kernel, first),
        out_shape=jax.ShapeDtypeStruct((slots, rows, groups * width), jnp.bfloat16),
        grid_spec=pltpu.PrefetchScalarGridSpec(
            num_scalar_prefetch=2,
            grid=(1,),
            in_specs=[hbm] * 5 + [pl.BlockSpec((1, groups * width), lambda i, *_: (0, 0))],
            out_specs=pl.BlockSpec((slots, rows, groups * width), lambda i, *_: (0, 0, 0)),
            scratch_shapes=[
                pltpu.VMEM((groups, slots, rows, width), jnp.bfloat16),
                pltpu.VMEM((groups, places, rows, width), jnp.bfloat16),
                pltpu.VMEM((groups, places, rows, width), jnp.bfloat16),
                pltpu.SemaphoreType.DMA((groups, 7)),
            ],
        ),
        compiler_params=pltpu.CompilerParams(vmem_limit_bytes=VMEM_LIMIT),
        cost_estimate=pl.CostEstimate(
            flops=4 * pairs * head_dim, bytes_accessed=12 * slots * rows * groups * width, transcendentals=pairs
        ),
        name="attention",
    )(neighbours, counts, queries, keys, values, *halo, gate_row)


def project_kernel(pieces_of, group_ref, own_hbm, sibling_hbm, *refs):
    n = sum(pieces_of)
    own_ref, sibling_ref, att_ref, wbuf, att_sem, in_sem = refs[n:]
    rows = own_hbm.shape[0]
    group = group_ref[0]
    begins, loads, at = [], [], 0
    for b, count in enumerate(pieces_of):
        begins.append(at)
        copies = []
        first = sum(pieces_of[:b])
        for i, piece in enumerate(refs[first : first + count]):
            high = piece.shape[0]
            start = begins[-1]
            if count == 2:
                start = start + (group if i == 0 else 1 - group) * high
            start = pl.multiple_of(start, high)
            copies.append(pltpu.make_async_copy(piece, wbuf.at[pl.ds(start, high)], in_sem.at[b, i]))
            at += high
        loads.append(copies)
    att_loads = [
        pltpu.make_async_copy(src, att_ref.at[pl.ds(i * rows, rows)], att_sem.at[i])
        for i, src in enumerate((own_hbm, sibling_hbm))
    ]
    for c in att_loads[:1] + loads[0] + att_loads[1:]:
        c.start()
    asked, arrived, done = 1, 0, 0
    while done < at:
        step = min(256, at - done)
        while arrived < len(loads) and begins[arrived] < done + step:
            for c in loads[arrived]:
                c.wait()
            arrived += 1
            if asked < len(loads):
                for c in loads[asked]:
                    c.start()
                asked += 1
        for i, ref in enumerate((own_ref, sibling_ref)):
            if done == 0:
                att_loads[i].wait()
            ref[:, done : done + step] = lax.dot_general(
                att_ref[i * rows : (i + 1) * rows],
                wbuf[done : done + step],
                (((1,), (1,)), ((), ())),
                preferred_element_type=jnp.float32,
            ).astype(ref.dtype)
        done += step


def project(own, sibling, blocks, group):
    rows, channels = own.shape
    pieces = [p for b in blocks for p in b]
    width = sum(p.shape[0] for p in pieces)
    padded = -(-width // 128) * 128
    hbm = pl.BlockSpec(memory_space=pl.ANY)
    limit = (32 if len(pieces) > 4 else 20) * 1024 * 1024
    result = jax.ShapeDtypeStruct((rows, padded), jnp.bfloat16)
    return pl.pallas_call(
        functools.partial(project_kernel, tuple(len(b) for b in blocks)),
        out_shape=(result, result),
        grid_spec=pltpu.PrefetchScalarGridSpec(
            num_scalar_prefetch=1,
            grid=(1,),
            in_specs=[hbm] * (2 + len(pieces)),
            out_specs=(pl.BlockSpec((rows, padded), lambda i, *_: (0, 0)),) * 2,
            scratch_shapes=[
                pltpu.VMEM((2 * rows, channels), jnp.bfloat16),
                pltpu.VMEM((width, channels), jnp.bfloat16),
                pltpu.SemaphoreType.DMA((2,)),
                pltpu.SemaphoreType.DMA((len(blocks), 2)),
            ],
        ),
        compiler_params=pltpu.CompilerParams(vmem_limit_bytes=limit),
        cost_estimate=pl.CostEstimate(
            flops=4 * rows * channels * width,
            bytes_accessed=2 * (channels * width + 2 * rows * (channels + width)),
            transcendentals=0,
        ),
        name="project",
    )(group.reshape(1), own, sibling, *pieces)


def assemble_kernel(places, shard, scalars, *refs):
    arrays, (out_ref, buf, sem) = refs[:-3], refs[-3:]
    half = shard // 2
    high = buf.shape[1]
    rows = pl.ds(pl.multiple_of(pl.program_id(0) * high, high), high)
    stores = []
    for b, parts in enumerate(places):

        def place(first_core, group):
            for c in range(CORES):
                for i, (array, lane) in enumerate(parts):
                    src = arrays[2 * array + (0 if c == first_core else 1)]
                    wide = shard if len(parts) == 1 else half
                    to = c * shard + (0 if len(parts) == 1 else (group if i == 0 else 1 - group) * half)
                    buf[b, :, to : to + wide] = src[:, lane : lane + wide]

        if len(parts) == 1:
            for c in range(CORES):
                pl.when(scalars[0] == c)(functools.partial(place, c, 0))
        else:
            for c in range(CORES):
                for g in range(2):
                    pl.when((scalars[0] == c) & (scalars[1] == g))(functools.partial(place, c, g))
        where = pl.ds(pl.multiple_of(scalars[2 + b] * CORES * shard, CORES * shard), CORES * shard)
        store = pltpu.make_async_copy(buf.at[b], out_ref.at[rows, where], sem.at[b])
        store.start()
        stores.append(store)
    for store in stores:
        store.wait()


def assemble(arrays, places, scalars, shard, columns):
    rows = arrays[0].shape[0]
    chunk = 128 if rows % 128 == 0 else rows
    return pl.pallas_call(
        functools.partial(assemble_kernel, places, shard),
        out_shape=jax.ShapeDtypeStruct((rows, columns), jnp.bfloat16),
        grid_spec=pltpu.PrefetchScalarGridSpec(
            num_scalar_prefetch=1,
            grid=(rows // chunk,),
            in_specs=[pl.BlockSpec((chunk, a.shape[1]), lambda i, *_: (i, 0)) for a in arrays],
            out_specs=pl.BlockSpec(memory_space=pltpu.HBM),
            scratch_shapes=[
                pltpu.VMEM((len(places), chunk, CORES * shard), jnp.bfloat16),
                pltpu.SemaphoreType.DMA((len(places),)),
            ],
        ),
        compiler_params=pltpu.CompilerParams(vmem_limit_bytes=20 * 1024 * 1024),
        cost_estimate=pl.CostEstimate(flops=0, bytes_accessed=4 * rows * columns, transcendentals=0),
        name="assemble",
    )(scalars, *arrays)


def on_device(groups, devices, queries, keys, values, counts, neighbours, gate_table, step, out_weight):
    slots, rows, channels = queries.shape
    shard = out_weight.shape[1]
    columns = shard * devices
    chips = devices // CORES
    length = chips // COLUMNS

    def permute(array, target):
        pairs = []
        for g in range(groups):
            for d in range(devices):
                to = target(g, d // (CORES * COLUMNS), d // CORES % COLUMNS, d % CORES)
                if to is not None:
                    tg, tz, tx, tc = to
                    pairs.append((g * devices + d, tg * devices + (tz * COLUMNS + tx) * CORES + tc))
        return lax.ppermute(array, ("groups", "dp"), pairs)

    def within_member(array, by):
        pairs = []
        for d in range(devices):
            first, second = (d, (d + by) % devices) if by > 0 else ((d + by) % devices, d)
            if (first - MEMBER_DEVS // 2) % MEMBER_DEVS != MEMBER_DEVS - 1:
                pairs.append((d, (d + by) % devices))
        return lax.ppermute(array, "dp", pairs)

    tail_start = jnp.maximum(counts[0] - HALO, 0)
    edges = [(lax.dynamic_slice_in_dim(a, tail_start, HALO, 0), a[:HALO]) for a in (keys, values)]
    gate_row = lax.dynamic_slice_in_dim(gate_table, step[0], 1, 0)
    weight = out_weight.T

    if not (groups == 2 and devices % (CORES * COLUMNS) == 0 and length >= 3 and shard % 32 == 0 and (CORES * shard) % 128 == 0):
        halo = [within_member(jnp.stack(e), by) for e, by in zip(zip(*edges), (1, -1))]
        att = attend(queries, keys, values, halo, neighbours.reshape(-1), counts, gate_row)
        full = lax.all_gather(weight, "dp", axis=0, tiled=True)
        mixed = lax.dot_general(
            att.reshape(slots * rows, channels), full, (((1,), (1,)), ((), ())), preferred_element_type=jnp.float32
        )
        return mixed.astype(jnp.bfloat16).reshape(slots, rows, columns)

    over = {
        "z": lambda g, z, x, c: (g, (z + 1) % length, x, c),
        "x": lambda g, z, x, c: (g, z, (x + 1) % COLUMNS, c),
        "y": lambda g, z, x, c: (1 - g, z, x, c),
        "s": lambda g, z, x, c: (g, z, x, 1 - c),
    }
    group = lax.axis_index("groups")
    device = lax.axis_index("dp")
    core = device % CORES
    my_x, my_z = device // CORES % COLUMNS, device // (CORES * COLUMNS)

    half = shard // 2
    have = {
        ("z", "p", 0): lax.dynamic_slice_in_dim(weight, group * half, half, 0),
        "weight": weight,
    }
    sends = {
        "z": [(("z", "p", s), ("z", "p", s + 1)) for s in range(length - 1)]
        + [(("z", "q", s), ("z", "q", s + 1)) for s in range(1, length - 1)],
        "x": [(("z", "p", s), ("x", "p", s)) for s in range(length)] + [(("z", "q", 0), ("x", "q", 0))],
        "y": [None, (("z", "p", 1), ("z", "q", 1))] + [(("x", "p", s), ("x", "q", s)) for s in range(1, length)],
    }
    rounds = max(len(v) for v in sends.values())
    every = [("z", s) for s in range(length)] + [("x", s) for s in range(length)]

    def names_of(b):
        return ["weight"] if b == ("z", 0) else [(b[0], h, b[1]) for h in "pq"]

    def chip_of(b):
        x = my_x if b[0] == "z" else (my_x + 1) % COLUMNS
        return (my_z - b[1]) % length * COLUMNS + x

    by_then = {"weight", ("z", "p", 0)} | {s[1] for link in sends.values() for s in link[: rounds - 1] if s}
    whole = [b for b in every if all(n in by_then for n in names_of(b))]
    halves = [b for b in every if b not in whole]
    scalars = jnp.stack([core, group] + [chip_of(b) for b in whole + halves]).astype(jnp.int32)
    small = [neighbours.reshape(-1), gate_row, scalars, group.reshape(1), weight]

    arrived, att, att_sibling, early = [], None, None, None
    for r in range(rounds):
        names = list(arrived)
        items = [(link, *sends[link][r]) for link in ("z", "x", "y") if r < len(sends[link]) and sends[link][r]]
        edge = [jnp.stack(e) for e in zip(*edges)] if r == HALO_ROUND else []
        bar = lax.optimization_barrier(
            ([have[n] for n in names], [have[src] for _, src, _ in items], att, att_sibling, edge, small if r else [])
        )
        for n, a in zip(names, bar[0]):
            have[n] = a
        _, sources, att, att_sibling, edge, small = (*bar[:5], bar[5] if r else small)
        arrived = []
        for (link, src, dst), a in zip(items, sources):
            have[dst] = permute(a, over[link])
            arrived.append(dst)
        for by, a in zip((1, -1), edge):
            have["halo", by] = within_member(a, by)
        if r == 1:
            have[("z", "q", 0)] = lax.dynamic_slice_in_dim(small[4], (1 - group) * half, half, 0)
            arrived.append(("z", "q", 0))
        if r == HALO_ROUND + 1:
            arrived += [("halo", by) for by in (1, -1)]
        if r == HALO_ROUND + 2:
            halo = [have["halo", by] for by in (1, -1)]
            att = attend(queries, keys, values, halo, small[0], counts, small[1])
            att = att.reshape(slots * rows, channels)
        elif r == HALO_ROUND + 3:
            att_sibling = permute(att, over["s"])
        if r == rounds - 1:
            pieces = [[have[n] for n in names_of(b)] for b in whole] + [[have[(b[0], "p", b[1])]] for b in halves]
            early = project(att, att_sibling, pieces, small[3])
    names = list(arrived)
    bar, early, att, att_sibling = lax.optimization_barrier(([have[n] for n in names], early, att, att_sibling))
    for n, a in zip(names, bar):
        have[n] = a
    early = [early[0], permute(early[1], over["s"])]
    late = project(att, att_sibling, [[have[(b[0], "q", b[1])]] for b in halves], small[3])
    late = [late[0], permute(late[1], over["s"])]
    at = len(whole) * shard
    places = tuple(((0, i * shard),) for i in range(len(whole)))
    places += tuple(((0, at + i * half), (1, i * half)) for i in range(len(halves)))
    out = assemble(early + late, places, small[2], shard, columns)
    return out.reshape(slots, rows, columns)


def solution(mesh):
    both = P(("groups", "dp"), None, None)
    placed = (both, both, both, P(("groups", "dp")), P(("groups", "dp"), None), P(), P(), P(None, "dp"))
    return jax.shard_map(
        functools.partial(on_device, mesh.shape["groups"], mesh.shape["dp"]),
        mesh=mesh,
        in_specs=placed,
        out_specs=both,
        check_vma=False,
    )
```

```python
import functools
import math

import jax
import jax.numpy as jnp
from jax import lax
from jax.experimental import pallas as pl
from jax.experimental.pallas import tpu as pltpu
from jax.sharding import PartitionSpec as P

HEADS = 20
HALO = 1
MEMBER_DEVS = 4
CORES = 2
COLUMNS = 2

masked_score = -1e30
HALO_ROUND = 1
VMEM_LIMIT = 60 * 1024 * 1024


def attention_kernel(first, index_ref, count_ref, q_hbm, k_hbm, v_hbm, before_hbm, after_hbm, gate_ref, o_ref, q_ref, ext_k, ext_v, sems):
    groups, slots, rows, width = q_ref.shape
    head_dim = q_hbm.shape[2] // HEADS
    places = slots + 2 * HALO
    picks = index_ref.shape[0] // slots
    to_exponent = math.log2(math.e) / math.sqrt(head_dim)

    def loads(g):
        at = pl.ds(pl.multiple_of((first + g) * width, width), width)
        pairs = [(q_hbm.at[:, :, at], q_ref.at[g])]
        for i, (own, ext) in enumerate(((k_hbm, ext_k), (v_hbm, ext_v))):
            pairs.append((before_hbm.at[i, :, :, at], ext.at[g, pl.ds(0, HALO)]))
            pairs.append((own.at[:, :, at], ext.at[g, pl.ds(HALO, slots)]))
            pairs.append((after_hbm.at[i, :, :, at], ext.at[g, pl.ds(HALO + slots, HALO)]))
        return [pltpu.make_async_copy(src, dst, sems.at[g, i]) for i, (src, dst) in enumerate(pairs)]

    for c in loads(0):
        c.start()

    def head_group(g, _):
        for c in loads(g):
            c.wait()

        @pl.when(g + 1 < groups)
        def _():
            for c in loads(g + 1):
                c.start()

        base = pl.multiple_of(g * width, width)
        for slot in range(slots):

            @pl.when(slot < count_ref[0])
            def _():
                place = [index_ref[slot * picks + j] for j in range(picks)]
                held = [jnp.minimum(p, places - 1) for p in place]
                ats = [pl.ds(h * head_dim, head_dim) for h in range(width // head_dim)]
                scored, weighed = [], []
                for at in ats:
                    query = q_ref[g, slot, :, at]
                    keyv = jnp.concatenate([ext_k[g, held[j], :, at] for j in range(picks)], axis=0)
                    scored.append(lax.dot_general(query, keyv, (((1,), (1,)), ((), ())), preferred_element_type=jnp.float32))
                for sc in scored:
                    sc = [jnp.where(place[j] < places, sc[:, j * rows : (j + 1) * rows], masked_score) for j in range(picks)]
                    top = jnp.max(functools.reduce(jnp.maximum, sc), axis=1, keepdims=True)
                    raw = [jnp.exp2((s - top) * to_exponent) for s in sc]
                    den = jnp.sum(functools.reduce(jnp.add, raw), axis=1, keepdims=True)
                    weighed.append((jnp.concatenate([r.astype(jnp.bfloat16) for r in raw], axis=1), den))
                for h, at in enumerate(ats):
                    out_at = pl.ds(pl.multiple_of(base + h * head_dim, head_dim), head_dim)
                    vals = jnp.concatenate([ext_v[g, held[j], :, at] for j in range(picks)], axis=0)
                    summed = jnp.dot(weighed[h][0], vals, preferred_element_type=jnp.float32)
                    o_ref[slot, :, out_at] = (summed * (1.0 / weighed[h][1]) * gate_ref[:, out_at]).astype(o_ref.dtype)

            @pl.when(slot >= count_ref[0])
            def _():
                o_ref[slot, :, pl.ds(base, width)] = jnp.zeros((rows, width), o_ref.dtype)

        return 0

    lax.fori_loop(0, groups, head_group, 0)


def attend(queries, keys, values, halo, neighbours, counts, gate_row, part=0, parts=1):
    slots, rows, channels = queries.shape
    head_dim = channels // HEADS
    heads = 4 if HEADS % 4 == 0 else 1
    width = heads * head_dim
    places = slots + 2 * HALO
    first, last = (-(-(HEADS // heads) * p // parts) for p in (part, part + 1))
    groups = last - first
    gate_row = gate_row[:, first * width : last * width]
    hbm = pl.BlockSpec(memory_space=pltpu.HBM)
    pairs = slots * groups * heads * rows * (neighbours.shape[0] // slots) * rows
    return pl.pallas_call(
        functools.partial(attention_kernel, first),
        out_shape=jax.ShapeDtypeStruct((slots, rows, groups * width), jnp.bfloat16),
        grid_spec=pltpu.PrefetchScalarGridSpec(
            num_scalar_prefetch=2,
            grid=(1,),
            in_specs=[hbm] * 5 + [pl.BlockSpec((1, groups * width), lambda i, *_: (0, 0))],
            out_specs=pl.BlockSpec((slots, rows, groups * width), lambda i, *_: (0, 0, 0)),
            scratch_shapes=[
                pltpu.VMEM((groups, slots, rows, width), jnp.bfloat16),
                pltpu.VMEM((groups, places, rows, width), jnp.bfloat16),
                pltpu.VMEM((groups, places, rows, width), jnp.bfloat16),
                pltpu.SemaphoreType.DMA((groups, 7)),
            ],
        ),
        compiler_params=pltpu.CompilerParams(vmem_limit_bytes=VMEM_LIMIT),
        cost_estimate=pl.CostEstimate(
            flops=4 * pairs * head_dim, bytes_accessed=12 * slots * rows * groups * width, transcendentals=pairs
        ),
        name="attention",
    )(neighbours, counts, queries, keys, values, *halo, gate_row)


def project_kernel(pieces_of, group_ref, own_hbm, sibling_hbm, *refs):
    n = sum(pieces_of)
    own_ref, sibling_ref, att_ref, wbuf, att_sem, in_sem = refs[n:]
    rows = own_hbm.shape[0]
    group = group_ref[0]
    begins, loads, at = [], [], 0
    for b, count in enumerate(pieces_of):
        begins.append(at)
        copies = []
        first = sum(pieces_of[:b])
        for i, piece in enumerate(refs[first : first + count]):
            high = piece.shape[0]
            start = begins[-1]
            if count == 2:
                start = start + (group if i == 0 else 1 - group) * high
            start = pl.multiple_of(start, high)
            copies.append(pltpu.make_async_copy(piece, wbuf.at[pl.ds(start, high)], in_sem.at[b, i]))
            at += high
        loads.append(copies)
    att_loads = [
        pltpu.make_async_copy(src, att_ref.at[pl.ds(i * rows, rows)], att_sem.at[i])
        for i, src in enumerate((own_hbm, sibling_hbm))
    ]
    for c in att_loads[:1] + loads[0] + att_loads[1:]:
        c.start()
    asked, arrived, done = 1, 0, 0
    while done < at:
        step = min(256, at - done)
        while arrived < len(loads) and begins[arrived] < done + step:
            for c in loads[arrived]:
                c.wait()
            arrived += 1
            if asked < len(loads):
                for c in loads[asked]:
                    c.start()
                asked += 1
        for i, ref in enumerate((own_ref, sibling_ref)):
            if done == 0:
                att_loads[i].wait()
            ref[:, done : done + step] = lax.dot_general(
                att_ref[i * rows : (i + 1) * rows],
                wbuf[done : done + step],
                (((1,), (1,)), ((), ())),
                preferred_element_type=jnp.float32,
            ).astype(ref.dtype)
        done += step


def project(own, sibling, blocks, group):
    rows, channels = own.shape
    pieces = [p for b in blocks for p in b]
    width = sum(p.shape[0] for p in pieces)
    padded = -(-width // 128) * 128
    hbm = pl.BlockSpec(memory_space=pl.ANY)
    limit = (32 if len(pieces) > 4 else 20) * 1024 * 1024
    result = jax.ShapeDtypeStruct((rows, padded), jnp.bfloat16)
    return pl.pallas_call(
        functools.partial(project_kernel, tuple(len(b) for b in blocks)),
        out_shape=(result, result),
        grid_spec=pltpu.PrefetchScalarGridSpec(
            num_scalar_prefetch=1,
            grid=(1,),
            in_specs=[hbm] * (2 + len(pieces)),
            out_specs=(pl.BlockSpec((rows, padded), lambda i, *_: (0, 0)),) * 2,
            scratch_shapes=[
                pltpu.VMEM((2 * rows, channels), jnp.bfloat16),
                pltpu.VMEM((width, channels), jnp.bfloat16),
                pltpu.SemaphoreType.DMA((2,)),
                pltpu.SemaphoreType.DMA((len(blocks), 2)),
            ],
        ),
        compiler_params=pltpu.CompilerParams(vmem_limit_bytes=limit),
        cost_estimate=pl.CostEstimate(
            flops=4 * rows * channels * width,
            bytes_accessed=2 * (channels * width + 2 * rows * (channels + width)),
            transcendentals=0,
        ),
        name="project",
    )(group.reshape(1), own, sibling, *pieces)


def assemble_kernel(places, shard, scalars, *refs):
    arrays, (out_ref, buf, sem) = refs[:-3], refs[-3:]
    half = shard // 2
    stores = []
    for b, parts in enumerate(places):

        def place(first_core, group):
            for c in range(CORES):
                for i, (array, lane) in enumerate(parts):
                    src = arrays[2 * array + (0 if c == first_core else 1)]
                    wide = shard if len(parts) == 1 else half
                    to = c * shard + (0 if len(parts) == 1 else (group if i == 0 else 1 - group) * half)
                    buf[b, :, to : to + wide] = src[:, lane : lane + wide]

        if len(parts) == 1:
            for c in range(CORES):
                pl.when(scalars[0] == c)(functools.partial(place, c, 0))
        else:
            for c in range(CORES):
                for g in range(2):
                    pl.when((scalars[0] == c) & (scalars[1] == g))(functools.partial(place, c, g))
        where = pl.ds(pl.multiple_of(scalars[2 + b] * CORES * shard, CORES * shard), CORES * shard)
        store = pltpu.make_async_copy(buf.at[b], out_ref.at[:, where], sem.at[b])
        store.start()
        stores.append(store)
    for store in stores:
        store.wait()


def assemble(arrays, places, scalars, shard, columns):
    rows = arrays[0].shape[0]
    return pl.pallas_call(
        functools.partial(assemble_kernel, places, shard),
        out_shape=jax.ShapeDtypeStruct((rows, columns), jnp.bfloat16),
        grid_spec=pltpu.PrefetchScalarGridSpec(
            num_scalar_prefetch=1,
            grid=(1,),
            in_specs=[pl.BlockSpec(a.shape, lambda i, *_: (0, 0)) for a in arrays],
            out_specs=pl.BlockSpec(memory_space=pltpu.HBM),
            scratch_shapes=[
                pltpu.VMEM((len(places), rows, CORES * shard), jnp.bfloat16),
                pltpu.SemaphoreType.DMA((len(places),)),
            ],
        ),
        compiler_params=pltpu.CompilerParams(vmem_limit_bytes=20 * 1024 * 1024),
        cost_estimate=pl.CostEstimate(flops=0, bytes_accessed=4 * rows * columns, transcendentals=0),
        name="assemble",
    )(scalars, *arrays)


def on_device(groups, devices, queries, keys, values, counts, neighbours, gate_table, step, out_weight):
    slots, rows, channels = queries.shape
    shard = out_weight.shape[1]
    columns = shard * devices
    chips = devices // CORES
    length = chips // COLUMNS

    def permute(array, target):
        pairs = []
        for g in range(groups):
            for d in range(devices):
                to = target(g, d // (CORES * COLUMNS), d // CORES % COLUMNS, d % CORES)
                if to is not None:
                    tg, tz, tx, tc = to
                    pairs.append((g * devices + d, tg * devices + (tz * COLUMNS + tx) * CORES + tc))
        return lax.ppermute(array, ("groups", "dp"), pairs)

    def within_member(array, by):
        pairs = []
        for d in range(devices):
            first, second = (d, (d + by) % devices) if by > 0 else ((d + by) % devices, d)
            if (first - MEMBER_DEVS // 2) % MEMBER_DEVS != MEMBER_DEVS - 1:
                pairs.append((d, (d + by) % devices))
        return lax.ppermute(array, "dp", pairs)

    tail_start = jnp.maximum(counts[0] - HALO, 0)
    edges = [(lax.dynamic_slice_in_dim(a, tail_start, HALO, 0), a[:HALO]) for a in (keys, values)]
    gate_row = lax.dynamic_slice_in_dim(gate_table, step[0], 1, 0)
    weight = out_weight.T

    if not (groups == 2 and devices % (CORES * COLUMNS) == 0 and length >= 3 and shard % 32 == 0 and (CORES * shard) % 128 == 0):
        halo = [within_member(jnp.stack(e), by) for e, by in zip(zip(*edges), (1, -1))]
        att = attend(queries, keys, values, halo, neighbours.reshape(-1), counts, gate_row)
        full = lax.all_gather(weight, "dp", axis=0, tiled=True)
        mixed = lax.dot_general(
            att.reshape(slots * rows, channels), full, (((1,), (1,)), ((), ())), preferred_element_type=jnp.float32
        )
        return mixed.astype(jnp.bfloat16).reshape(slots, rows, columns)

    over = {
        "z": lambda g, z, x, c: (g, (z + 1) % length, x, c),
        "x": lambda g, z, x, c: (g, z, (x + 1) % COLUMNS, c),
        "y": lambda g, z, x, c: (1 - g, z, x, c),
        "s": lambda g, z, x, c: (g, z, x, 1 - c),
    }
    group = lax.axis_index("groups")
    device = lax.axis_index("dp")
    core = device % CORES
    my_x, my_z = device // CORES % COLUMNS, device // (CORES * COLUMNS)

    half = shard // 2
    have = {
        ("z", "p", 0): lax.dynamic_slice_in_dim(weight, group * half, half, 0),
        "weight": weight,
    }
    sends = {
        "z": [(("z", "p", s), ("z", "p", s + 1)) for s in range(length - 1)]
        + [(("z", "q", s), ("z", "q", s + 1)) for s in range(1, length - 1)],
        "x": [(("z", "p", s), ("x", "p", s)) for s in range(length)] + [(("z", "q", 0), ("x", "q", 0))],
        "y": [None, (("z", "p", 1), ("z", "q", 1))] + [(("x", "p", s), ("x", "q", s)) for s in range(1, length)],
    }
    rounds = max(len(v) for v in sends.values())
    every = [("z", s) for s in range(length)] + [("x", s) for s in range(length)]

    def names_of(b):
        return ["weight"] if b == ("z", 0) else [(b[0], h, b[1]) for h in "pq"]

    def chip_of(b):
        x = my_x if b[0] == "z" else (my_x + 1) % COLUMNS
        return (my_z - b[1]) % length * COLUMNS + x

    by_then = {"weight", ("z", "p", 0)} | {s[1] for link in sends.values() for s in link[: rounds - 1] if s}
    whole = [b for b in every if all(n in by_then for n in names_of(b))]
    halves = [b for b in every if b not in whole]
    scalars = jnp.stack([core, group] + [chip_of(b) for b in whole + halves]).astype(jnp.int32)
    small = [neighbours.reshape(-1), gate_row, scalars, group.reshape(1), weight]

    arrived, att, att_sibling, early = [], None, None, None
    for r in range(rounds):
        names = list(arrived)
        items = [(link, *sends[link][r]) for link in ("z", "x", "y") if r < len(sends[link]) and sends[link][r]]
        edge = [jnp.stack(e) for e in zip(*edges)] if r == HALO_ROUND else []
        bar = lax.optimization_barrier(
            ([have[n] for n in names], [have[src] for _, src, _ in items], att, att_sibling, edge, small if r else [])
        )
        for n, a in zip(names, bar[0]):
            have[n] = a
        _, sources, att, att_sibling, edge, small = (*bar[:5], bar[5] if r else small)
        arrived = []
        for (link, src, dst), a in zip(items, sources):
            have[dst] = permute(a, over[link])
            arrived.append(dst)
        for by, a in zip((1, -1), edge):
            have["halo", by] = within_member(a, by)
        if r == 1:
            have[("z", "q", 0)] = lax.dynamic_slice_in_dim(small[4], (1 - group) * half, half, 0)
            arrived.append(("z", "q", 0))
        if r == HALO_ROUND + 1:
            arrived += [("halo", by) for by in (1, -1)]
        if r == HALO_ROUND + 2:
            halo = [have["halo", by] for by in (1, -1)]
            att = attend(queries, keys, values, halo, small[0], counts, small[1])
            att = att.reshape(slots * rows, channels)
        elif r == HALO_ROUND + 3:
            att_sibling = permute(att, over["s"])
        if r == rounds - 1:
            pieces = [[have[n] for n in names_of(b)] for b in whole] + [[have[(b[0], "p", b[1])]] for b in halves]
            early = project(att, att_sibling, pieces, small[3])
    names = list(arrived)
    bar, early, att, att_sibling = lax.optimization_barrier(([have[n] for n in names], early, att, att_sibling))
    for n, a in zip(names, bar):
        have[n] = a
    early = [early[0], permute(early[1], over["s"])]
    late = project(att, att_sibling, [[have[(b[0], "q", b[1])]] for b in halves], small[3])
    late = [late[0], permute(late[1], over["s"])]
    at = len(whole) * shard
    places = tuple(((0, i * shard),) for i in range(len(whole)))
    places += tuple(((0, at + i * half), (1, i * half)) for i in range(len(halves)))
    out = assemble(early + late, places, small[2], shard, columns)
    return out.reshape(slots, rows, columns)


def solution(mesh):
    both = P(("groups", "dp"), None, None)
    placed = (both, both, both, P(("groups", "dp")), P(("groups", "dp"), None), P(), P(), P(None, "dp"))
    return jax.shard_map(
        functools.partial(on_device, mesh.shape["groups"], mesh.shape["dp"]),
        mesh=mesh,
        in_specs=placed,
        out_specs=both,
        check_vma=False,
    )
```
